32 devices in a mesh: dp: 16 (over z, y, x), mp: 2 (over core).
Axes of the slice: x: 2, y: 2, z: 4, core: 2. Of those that a mesh axis runs over, the one named last changes fastest.
Arguments:
- inputs: bfloat16 [8192, 3072], P('dp', 'mp'), may hold values from -6 to 6
- queries: bfloat16 [8192, 3072], P('dp', 'mp'), may hold values from -5 to 5
- keys: bfloat16 [8192, 3072], P('dp', 'mp'), may hold values from -5 to 5
- values: bfloat16 [8192, 3072], P('dp', 'mp'), may hold values from -16 to 16
- out_weight: bfloat16 [3072, 3072], P('dp', 'mp'), may hold values from -0.109375 to 0.109375
Outputs:
- block_out: bfloat16 [8192, 3072], P('dp', 'mp')
The draws below stay inside these ranges and needn't reach their ends.
All inputs are finite; a program needn't handle non-finite values.
Results may differ from the reference program's by a relative error of at most 0.0034.
Values may be sent and summed in bfloat16 or wider, within the bound.
A program may use at most 64 MiB of HBM per device.

```python
import math
import jax
import jax.numpy as jnp
from jax import lax

HEAD_DIM = 128
OUT_FEAT = 3072
PATCHES = 256
ATTN = 3072
IMAGES = 32
TOKENS = 8192


def draw_queries(key, part):
    own_key = jax.random.fold_in(key, 11)
    base = jax.random.truncated_normal(own_key, -4.0, 4.0, (TOKENS, ATTN), jnp.float32)
    return base.astype(jnp.bfloat16)


def draw_keys(key, part):
    own_key = jax.random.fold_in(key, 23)
    base = jax.random.truncated_normal(own_key, -4.0, 4.0, (TOKENS, ATTN), jnp.float32)
    return base.astype(jnp.bfloat16)


def level_of(key, dims, shards, low, top_value):
    def one(axis_at, shards_of):
        heights = jax.random.uniform(jax.random.fold_in(jax.random.fold_in(key, 6), axis_at), (shards_of,), jnp.float32, low / len(shards), top_value / len(shards))
        return jnp.repeat(jnp.exp(heights), dims[axis_at] // shards_of).reshape((-1,) + (1,) * (len(dims) - axis_at - 1))

    level = one(*shards[0])
    for cut in shards[1:]:
        level = level * one(*cut)
    return level


def noise(rng, extent, width, limit, shards=(), kind=jnp.bfloat16):
    entries = width * jax.random.normal(rng, extent, jnp.float32)
    if shards:
        entries = entries * level_of(rng, extent, shards, -0.22, 0.18)
    return jnp.clip(entries, -limit, limit).astype(kind)


def setup_inputs(seed: int = 0) -> dict:
    key_of = jax.random.split(jax.random.key(seed), 6)
    inputs = noise(key_of[0], (TOKENS, OUT_FEAT), 1.0, 6.0, ((0, 16), (1, 2)))
    queries = draw_queries(jax.random.fold_in(key_of[5], 71), 0)
    keys = draw_keys(jax.random.fold_in(key_of[5], 71), 0)
    values = noise(key_of[3], (TOKENS, ATTN), 3.0, 16.0, ((0, 16), (1, 2)))
    out_weight = noise(key_of[4], (ATTN, OUT_FEAT), ATTN ** -0.5, 0.109375, ((0, 16), (1, 2)))
    return dict(inputs=inputs, queries=queries, keys=keys, values=values, out_weight=out_weight)


def attend_image(query_img, key_img, value_img):
    head_count = query_img.shape[1] // HEAD_DIM
    query_heads = query_img.reshape(PATCHES, head_count, HEAD_DIM).astype(jnp.float32)
    key_heads = key_img.reshape(PATCHES, head_count, HEAD_DIM).astype(jnp.float32)
    value_heads = value_img.reshape(PATCHES, head_count, HEAD_DIM).astype(jnp.float32)
    scores = jnp.einsum('qhd,khd->hqk', query_heads, key_heads) / math.sqrt(HEAD_DIM)
    row_max = lax.optimization_barrier(jnp.max(scores, axis=-1, keepdims=True))
    shifted = jnp.exp(scores - row_max)
    probs = (shifted / lax.optimization_barrier(jnp.sum(shifted, axis=-1, keepdims=True))).astype(jnp.bfloat16)
    attended = jnp.einsum('hqk,khd->qhd', probs.astype(jnp.float32), value_heads)
    return attended.reshape(PATCHES, head_count * HEAD_DIM).astype(jnp.bfloat16)

def reference(inputs, queries, keys, values, out_weight):

    def one_image(index):
        start = (index * PATCHES).astype(jnp.int32)
        query_img = lax.dynamic_slice_in_dim(queries, start, PATCHES, 0)
        key_img = lax.dynamic_slice_in_dim(keys, start, PATCHES, 0)
        value_img = lax.dynamic_slice_in_dim(values, start, PATCHES, 0)
        return attend_image(query_img, key_img, value_img)
    attended = lax.map(one_image, jnp.arange(IMAGES, dtype=jnp.int32)).reshape(TOKENS, ATTN)
    projected = jnp.dot(attended, out_weight, preferred_element_type=jnp.float32)
    return (inputs.astype(jnp.float32) + projected).astype(jnp.bfloat16)
```

```python
import functools
import math

import jax
import jax.numpy as jnp
from jax import lax
from jax.experimental import pallas as pl
from jax.experimental.pallas import tpu as pltpu
from jax.sharding import PartitionSpec as P

HEAD_DIM = 128
PATCHES = 256
MESH = pl.DeviceIdType.MESH

PARTS = (("zxy", 0, 1), ("zyx", 1, 1), ("xzy", 2, 2), ("yzx", 4, 2))
GROUPS = 12
HEAD_START = 4


def hops(order, rx, ry, dz):
    diff = {"x": rx, "y": ry, "z": dz}
    last = max([i for i in range(3) if diff[order[i]]], default=-1)
    out = []
    if last >= 0 and order[last] == "z":
        out.append("u" if dz < 0 else "d")
    for axis in order[last + 1:]:
        out.extend(("u", "d") if axis == "z" else (axis,))
    return out


def arrivals(deep):
    chips = [(x, y, z) for z in range(deep) for y in range(2) for x in range(2)]
    ready, busy, when = [], {}, {}
    for c in chips:
        for rank, p in enumerate(range(len(PARTS))):
            ready.append((0.0, rank, c, p, c))
    while ready:
        ready.sort()
        now, rank, c, p, s = ready.pop(0)
        order, _, size = PARTS[p]
        rx, ry, dz = c[0] ^ s[0], c[1] ^ s[1], s[2] - c[2]
        if c != s:
            when.setdefault((p, rx, ry, dz), []).append(now)
        for hop in hops(order, rx, ry, dz):
            to = {
                "x": (1 - c[0], c[1], c[2]), "y": (c[0], 1 - c[1], c[2]),
                "u": (c[0], c[1], c[2] + 1), "d": (c[0], c[1], c[2] - 1),
            }[hop]
            if 0 <= to[2] < deep:
                end = max(now, busy.get((c, hop), 0.0)) + size
                busy[(c, hop)] = end
                ready.append((end + 0.3, rank, to, p, s))
    return sorted(when, key=lambda e: (sum(when[e]) / len(when[e]), e))


def kernel(deep, x_hbm, q_hbm, k_hbm, v_hbm, w_hbm, o_hbm,
           wbuf, xin, qv, kv, vv, att, acc, obuf,
           recv, sent, local, att_sent, att_recv):
    me, half = lax.axis_index("dp"), lax.axis_index("mp")
    x, y, z = me % 2, (me // 2) % 2, me // 4
    rows, width = w_hbm.shape
    tokens = q_hbm.shape[0]
    images, heads = tokens // PATCHES, width // HEAD_DIM
    sixth = rows // 6

    def index_of(cx, cy, cz):
        return (cz * 2 + cy) * 2 + cx

    near = {
        "x": index_of(1 - x, y, z), "y": index_of(x, 1 - y, z),
        "u": index_of(x, y, z + 1), "d": index_of(x, y, z - 1),
    }
    open_way = {"x": None, "y": None, "u": z < deep - 1, "d": z > 0}
    lane = {"x": 0, "y": 1, "u": 2, "d": 3}

    def maybe(cond, fn):
        if cond is None:
            fn()
        else:
            pl.when(cond)(fn)

    loads = [
        pltpu.make_async_copy(a, b, local.at[i])
        for i, (a, b) in enumerate(((q_hbm, qv), (k_hbm, kv), (v_hbm, vv), (x_hbm, xin)))
    ]
    own = pl.ds(pl.multiple_of(me * rows, 16), rows)
    loads.append(pltpu.make_async_copy(w_hbm, wbuf.at[own], local.at[4]))
    for load in loads:
        load.start()

    barrier = pltpu.get_barrier_semaphore()
    pl.semaphore_signal(barrier, inc=1, device_id=(me, 1 - half), device_id_type=MESH)
    for hop in "xyud":
        def greet(hop=hop):
            pl.semaphore_signal(barrier, inc=1, device_id=(near[hop], half), device_id_type=MESH)
        maybe(open_way[hop], greet)
    pl.semaphore_wait(barrier, 3 + jnp.minimum(z, 1) + jnp.minimum(deep - 1 - z, 1))

    def piece(p, source):
        _, first, size = PARTS[p]
        return wbuf.at[pl.ds(pl.multiple_of(source * rows + first * sixth, 16), size * sixth)]

    def copy(p, source, hop, src=None):
        spot = piece(p, source)
        return pltpu.make_async_remote_copy(
            src_ref=spot if src is None else src,
            dst_ref=spot,
            send_sem=sent.at[lane[hop]],
            recv_sem=recv.at[p, source],
            device_id=(near[hop], half),
            device_id_type=MESH,
        )

    first_sends = []
    for p, (order, first, size) in enumerate(PARTS):
        for hop in hops(order, 0, 0, 0):
            axis = "z" if hop in "ud" else hop
            first_sends.append((order.index(axis), p, hop))
    for _, p, hop in sorted(first_sends):
        _, first, size = PARTS[p]
        src = w_hbm.at[pl.ds(first * sixth, size * sixth)]
        maybe(open_way[hop], lambda p=p, hop=hop, src=src: copy(p, me, hop, src).start())

    def event(p, rx, ry, dz):
        source = index_of((x + rx) % 2, (y + ry) % 2, z + dz)

        def handle():
            copy(p, source, "x").wait_recv()
            for hop in hops(PARTS[p][0], rx, ry, dz):
                maybe(open_way[hop], lambda hop=hop: copy(p, source, hop).start())

        cond = None if dz == 0 else (z + dz < deep if dz > 0 else z + dz >= 0)
        maybe(cond, handle)

    def attend(unit):
        r = pl.multiple_of((unit // heads) * PATCHES, PATCHES)
        c = pl.multiple_of((unit % heads) * HEAD_DIM, HEAD_DIM)
        here = (pl.ds(r, PATCHES), pl.ds(c, HEAD_DIM))
        s = lax.dot_general(qv[here], kv[here], (((1,), (1,)), ((), ())), preferred_element_type=jnp.float32)
        s = s * (1.0 / math.sqrt(HEAD_DIM))
        e = jnp.exp(s - jnp.max(s, axis=-1, keepdims=True))
        probs = (e / jnp.sum(e, axis=-1, keepdims=True)).astype(jnp.bfloat16)
        a = jnp.dot(probs, vv[here], preferred_element_type=jnp.float32)
        att[pl.ds(r, PATCHES), pl.ds(pl.multiple_of(half * width + c, HEAD_DIM), HEAD_DIM)] = a.astype(jnp.bfloat16)

    def share(image):
        spot = att.at[pl.ds(image * PATCHES, PATCHES), pl.ds(pl.multiple_of(half * width, HEAD_DIM), width)]
        return pltpu.make_async_remote_copy(
            src_ref=spot, dst_ref=spot, send_sem=att_sent.at[image], recv_sem=att_recv.at[image],
            device_id=(me, 1 - half), device_id_type=MESH,
        )

    block, tile = 4 * rows, 256

    def project(dz):
        depth = pl.ds(pl.multiple_of((z + dz) * block, HEAD_DIM), block)

        def run():
            @pl.loop(0, width // tile)
            def _(i):
                cols = pl.ds(pl.multiple_of(i * tile, tile), tile)
                start = xin[:, cols].astype(jnp.float32) if dz == 0 else acc[:, cols]
                acc[:, cols] = start + jnp.dot(att[:, depth], wbuf[depth, cols], preferred_element_type=jnp.float32)

        maybe(None if dz == 0 else (z + dz < deep if dz > 0 else z + dz >= 0), run)

    order = arrivals(deep)
    for load in loads[:3]:
        load.wait()

    units = images * heads
    step = units // GROUPS
    early = 2 * len(order) // 3
    done = 0
    shared = 0
    for g in range(GROUPS):
        pl.loop(g * step, (g + 1) * step)(attend)
        while shared < images and (g + 1) * step >= (shared + 1) * heads:
            share(shared).start()
            shared += 1
        if g + 1 > HEAD_START:
            upto = early * (g + 1 - HEAD_START) // (GROUPS - HEAD_START)
            for e in order[done:upto]:
                event(*e)
            done = upto
    for load in loads[3:]:
        load.wait()
    for image in range(images):
        share(image).wait_recv()

    left = {}
    for e in order[done:]:
        left[e[3]] = left.get(e[3], 0) + 1
    for dz in sorted({e[3] for e in order}, key=lambda d: (abs(d), d)):
        if dz not in left:
            project(dz)
    for e in order[done:]:
        event(*e)
        left[e[3]] -= 1
        if left[e[3]] == 0:
            project(e[3])

    outs = []
    for i in range(width // tile):
        cols = pl.ds(i * tile, tile)
        obuf[:, cols] = acc[:, cols].astype(jnp.bfloat16)
        out = pltpu.make_async_copy(obuf.at[:, cols], o_hbm.at[:, cols], local.at[5 + i])
        out.start()
        outs.append(out)

    def drain(hop, count):
        spot = wbuf.at[pl.ds(0, count)]
        pltpu.make_async_remote_copy(
            src_ref=spot, dst_ref=spot, send_sem=sent.at[lane[hop]], recv_sem=recv.at[0, 0],
            device_id=(near[hop], half), device_id_type=MESH,
        ).wait_send()

    carried = {hop: {} for hop in "xyud"}
    for p, (name, _, size) in enumerate(PARTS):
        for at in range(deep):
            for rx in range(2):
                for ry in range(2):
                    for dz in range(-at, deep - at):
                        for hop in hops(name, rx, ry, dz):
                            if (hop == "u" and at == deep - 1) or (hop == "d" and at == 0):
                                continue
                            carried[hop][at] = carried[hop].get(at, 0) + size * sixth
    for hop in "xyud":
        for at, count in carried[hop].items():
            pl.when(z == at)(functools.partial(drain, hop, count))
    for image in range(images):
        share(image).wait_send()
    for out in outs:
        out.wait()


def fused(deep, inputs, queries, keys, values, out_weight):
    tokens, width = queries.shape
    rows = out_weight.shape[0]
    whole = 4 * deep * rows
    bf16, f32 = jnp.bfloat16, jnp.float32
    return pl.pallas_call(
        functools.partial(kernel, deep),
        out_shape=jax.ShapeDtypeStruct((tokens, width), bf16),
        in_specs=[pl.BlockSpec(memory_space=pl.ANY)] * 5,
        out_specs=pl.BlockSpec(memory_space=pl.ANY),
        scratch_shapes=[
            pltpu.VMEM((whole, width), bf16),
            pltpu.VMEM((tokens, width), bf16),
            pltpu.VMEM((tokens, width), bf16),
            pltpu.VMEM((tokens, width), bf16),
            pltpu.VMEM((tokens, width), bf16),
            pltpu.VMEM((tokens, whole), bf16),
            pltpu.VMEM((tokens, width), f32),
            pltpu.VMEM((tokens, width), bf16),
            pltpu.SemaphoreType.DMA((len(PARTS), 4 * deep)),
            pltpu.SemaphoreType.DMA((4,)),
            pltpu.SemaphoreType.DMA((5 + width // 256,)),
            pltpu.SemaphoreType.DMA((tokens // PATCHES,)),
            pltpu.SemaphoreType.DMA((tokens // PATCHES,)),
        ],
        compiler_params=pltpu.CompilerParams(
            collective_id=0, has_side_effects=True, vmem_limit_bytes=48 * 1024 * 1024
        ),
    )(inputs, queries, keys, values, out_weight)


def general(inputs, queries, keys, values, out_weight):
    tok_rows, local_width = queries.shape
    head_count = local_width // HEAD_DIM
    images = tok_rows // PATCHES
    split_shape = (images, PATCHES, head_count, HEAD_DIM)
    gathered = lax.all_gather(out_weight, "dp", axis=0, tiled=True)
    scores = jnp.einsum(
        "bqhd,bkhd->bhqk",
        queries.reshape(split_shape),
        keys.reshape(split_shape),
        preferred_element_type=jnp.float32,
    ) / math.sqrt(HEAD_DIM)
    row_max = jnp.max(scores, axis=-1, keepdims=True)
    shifted = jnp.exp(scores - row_max)
    probs = (shifted / jnp.sum(shifted, axis=-1, keepdims=True)).astype(jnp.bfloat16)
    attended = jnp.einsum(
        "bhqk,bkhd->bqhd", probs, values.reshape(split_shape), preferred_element_type=jnp.float32
    )
    attended = attended.astype(jnp.bfloat16).reshape(tok_rows, local_width)
    all_heads = lax.all_gather(attended, "mp", axis=1, tiled=True)
    projected = jnp.dot(all_heads, gathered, preferred_element_type=jnp.float32)
    return (inputs.astype(jnp.float32) + projected).astype(jnp.bfloat16)


def solution(mesh):
    parts, halves = mesh.shape["dp"], mesh.shape["mp"]

    def shards(inputs, queries, keys, values, out_weight):
        rows, width = out_weight.shape
        tokens = queries.shape[0]
        if (parts % 4 == 0 and 4 < parts <= 32 and halves == 2 and rows % 96 == 0 and width % 256 == 0
                and (tokens // PATCHES) * (width // HEAD_DIM) % GROUPS == 0):
            return fused(parts // 4, inputs, queries, keys, values, out_weight)
        return general(inputs, queries, keys, values, out_weight)

    return jax.shard_map(
        shards,
        mesh=mesh,
        in_specs=(P("dp", "mp"),) * 5,
        out_specs=P("dp", "mp"),
        check_vma=False,
    )
```

```python
import functools
import math

import jax
import jax.numpy as jnp
from jax import lax
from jax.experimental import pallas as pl
from jax.experimental.pallas import tpu as pltpu
from jax.sharding import PartitionSpec as P

HEAD_DIM = 128
PATCHES = 256
MESH = pl.DeviceIdType.MESH

PARTS = (("zxy", 3), ("zyx", 3), ("xzy", 3), ("yzx", 3))
GROUPS = 12
HEAD_START = 4
EARLY = (1, 2)
OWN_LATE = 0.0


def hops(order, rx, ry, k, place, deep):
    diff = {"x": rx, "y": ry, "z": k}
    last = max([i for i in range(3) if diff[order[i]]], default=-1)
    out = []
    if last >= 0 and order[last] == "z":
        out.append("i" if k < 0 else "o")
    for axis in order[last + 1:]:
        out.extend(("i", "o") if axis == "z" else (axis,))
    return [hop for hop in out if hop != "o" or place > 0]


def arrivals(deep):
    chips = [(x, y, z) for z in range(deep) for y in range(2) for x in range(2)]
    ready, busy, when = [], {}, [{} for _ in range(deep // 2)]
    for c in chips:
        for p in range(len(PARTS)):
            ready.append((0.0, p, c, c, ""))
    while ready:
        ready.sort()
        now, p, c, s, only = ready.pop(0)
        order, size = PARTS[p]
        inward = 1 if c[2] < deep // 2 else -1
        place = min(c[2], deep - 1 - c[2])
        rx, ry, k = c[0] ^ s[0], c[1] ^ s[1], (s[2] - c[2]) * inward
        if OWN_LATE and c == s and not only:
            ready.append((OWN_LATE, p, c, s, order[2]))
        if c != s:
            when[place].setdefault((p, rx, ry, k), []).append(now)
        for hop in hops(order, rx, ry, k, place, deep):
            if OWN_LATE and c == s and (only != hop if only else hop == order[2]):
                continue
            to = {
                "x": (1 - c[0], c[1], c[2]), "y": (c[0], 1 - c[1], c[2]),
                "i": (c[0], c[1], c[2] + inward), "o": (c[0], c[1], c[2] - inward),
            }[hop]
            end = max(now, busy.get((c, hop), 0.0)) + size
            busy[(c, hop)] = end
            ready.append((end + 0.3, p, to, s, ""))
    orders = [sorted(w, key=lambda e, w=w: (sum(w[e]) / len(w[e]), e)) for w in when]
    late = [sum(sum(w[e]) / len(w[e]) < OWN_LATE for e in w) for w in when]
    return orders, late


def kernel(deep, x_hbm, q_hbm, k_hbm, v_hbm, w_hbm, o_hbm,
           wbuf, xin, qv, kv, vv, att, acc, obuf,
           recv, sent, local, att_sent, att_recv):
    me, half = lax.axis_index("dp"), lax.axis_index("mp")
    x, y, z = me % 2, (me // 2) % 2, me // 4
    rows, width = w_hbm.shape
    tokens = q_hbm.shape[0]
    images, heads = tokens // PATCHES, width // HEAD_DIM
    unit_rows = rows // 12
    firsts = [sum(size for _, size in PARTS[:p]) for p in range(len(PARTS))]
    places = deep // 2
    lower = z < places
    inward = jnp.where(lower, 1, -1)
    place = jnp.where(lower, z, deep - 1 - z)

    def index_of(cx, cy, cz):
        return (cz * 2 + cy) * 2 + cx

    near = {
        "x": index_of(1 - x, y, z), "y": index_of(x, 1 - y, z),
        "i": index_of(x, y, z + inward), "o": index_of(x, y, z - inward),
    }
    lane = {"x": 0, "y": 1, "i": 2, "o": 3}

    loads = [
        pltpu.make_async_copy(a, b, local.at[i])
        for i, (a, b) in enumerate(((q_hbm, qv), (k_hbm, kv), (v_hbm, vv), (x_hbm, xin)))
    ]
    own = pl.ds(pl.multiple_of(me * rows, 16), rows)
    loads.append(pltpu.make_async_copy(w_hbm, wbuf.at[own], local.at[4]))
    for load in loads:
        load.start()

    barrier = pltpu.get_barrier_semaphore()
    pl.semaphore_signal(barrier, inc=1, device_id=(me, 1 - half), device_id_type=MESH)
    for hop in "xyi":
        pl.semaphore_signal(barrier, inc=1, device_id=(near[hop], half), device_id_type=MESH)

    @pl.when(place > 0)
    def _():
        pl.semaphore_signal(barrier, inc=1, device_id=(near["o"], half), device_id_type=MESH)

    pl.semaphore_wait(barrier, 4 + jnp.minimum(place, 1))

    def piece(p, source):
        first = pl.multiple_of(source * rows + firsts[p] * unit_rows, 16)
        return wbuf.at[pl.ds(first, PARTS[p][1] * unit_rows)]

    def copy(p, source, hop, src=None):
        spot = piece(p, source)
        return pltpu.make_async_remote_copy(
            src_ref=spot if src is None else src,
            dst_ref=spot,
            send_sem=sent.at[lane[hop]],
            recv_sem=recv.at[p, source],
            device_id=(near[hop], half),
            device_id_type=MESH,
        )

    first_sends = []
    for p, (name, _) in enumerate(PARTS):
        for hop in hops(name, 0, 0, 0, 1, deep):
            first_sends.append((name.index("z" if hop in "io" else hop), p, hop))
    for _, p, hop in sorted(first_sends):
        src = w_hbm.at[pl.ds(firsts[p] * unit_rows, PARTS[p][1] * unit_rows)]
        send = copy(p, me, hop, src)
        if OWN_LATE and PARTS[p][0].index("z" if hop in "io" else hop) == 2:
            continue
        if hop == "o":
            pl.when(place > 0)(send.start)
        else:
            send.start()

    orders, late = arrivals(deep)
    seen = [0] * places

    def event(at, p, rx, ry, k):
        source = index_of((x + rx) % 2, (y + ry) % 2, z + inward * k)
        if OWN_LATE and seen[at] == late[at]:
            for own_p, (name, _) in enumerate(PARTS):
                copy(own_p, me, name[2]).start()
        seen[at] += 1
        copy(p, source, "x").wait_recv()
        for hop in hops(PARTS[p][0], rx, ry, k, at, deep):
            copy(p, source, hop).start()

    def attend(unit):
        r = pl.multiple_of((unit // heads) * PATCHES, PATCHES)
        c = pl.multiple_of((unit % heads) * HEAD_DIM, HEAD_DIM)
        here = (pl.ds(r, PATCHES), pl.ds(c, HEAD_DIM))
        s = lax.dot_general(qv[here], kv[here], (((1,), (1,)), ((), ())), preferred_element_type=jnp.float32)
        s = s * (1.0 / math.sqrt(HEAD_DIM))
        e = jnp.exp(s - jnp.max(s, axis=-1, keepdims=True))
        probs = (e / jnp.sum(e, axis=-1, keepdims=True)).astype(jnp.bfloat16)
        a = jnp.dot(probs, vv[here], preferred_element_type=jnp.float32)
        att[pl.ds(r, PATCHES), pl.ds(pl.multiple_of(half * width + c, HEAD_DIM), HEAD_DIM)] = a.astype(jnp.bfloat16)

    def share(image):
        spot = att.at[pl.ds(image * PATCHES, PATCHES), pl.ds(pl.multiple_of(half * width, HEAD_DIM), width)]
        return pltpu.make_async_remote_copy(
            src_ref=spot, dst_ref=spot, send_sem=att_sent.at[image], recv_sem=att_recv.at[image],
            device_id=(me, 1 - half), device_id_type=MESH,
        )

    block, tile = 4 * rows, 256

    def project(k, last):
        depth = pl.ds(pl.multiple_of((z + inward * k) * block, HEAD_DIM), block)

        @pl.loop(0, width // tile)
        def _(i):
            cols = pl.ds(pl.multiple_of(i * tile, tile), tile)
            start = xin[:, cols].astype(jnp.float32) if k == 0 else acc[:, cols]
            total = start + jnp.dot(att[:, depth], wbuf[depth, cols], preferred_element_type=jnp.float32)
            if last:
                obuf[:, cols] = total.astype(jnp.bfloat16)
                pltpu.make_async_copy(obuf.at[:, cols], o_hbm.at[:, cols], local.at[5 + i]).start()
            else:
                acc[:, cols] = total

    for load in loads[:3] + loads[4:]:
        load.wait()

    units = images * heads
    step = units // GROUPS
    early = [len(order) * EARLY[0] // EARLY[1] for order in orders]
    done = [0] * places
    shared = 0
    for g in range(GROUPS):
        pl.loop(g * step, (g + 1) * step)(attend)
        while shared < images and (g + 1) * step >= (shared + 1) * heads:
            share(shared).start()
            shared += 1
        if g + 1 > HEAD_START:
            for at in range(places):
                upto = early[at] * (g + 1 - HEAD_START) // (GROUPS - HEAD_START)

                @pl.when(place == at)
                def _(at=at, upto=upto):
                    for e in orders[at][done[at]:upto]:
                        event(at, *e)
                done[at] = upto
    loads[3].wait()
    for image in range(images):
        share(image).wait_recv()

    def finish(at):
        rest = orders[at][done[at]:]
        final = {k: max([i for i, e in enumerate(rest) if e[3] == k], default=-1) for k in {e[3] for e in orders[at]}}
        planes = sorted(final, key=lambda k: (final[k], abs(k)))
        planes.remove(0)
        planes.insert(0, 0)
        for k in planes:
            final[k] = max(final[k], final[0])
        at_event = 0
        for k in planes:
            for e in rest[at_event:final[k] + 1]:
                event(at, *e)
            at_event = max(at_event, final[k] + 1)
            project(k, k == planes[-1])

    for at in range(places):
        pl.when(place == at)(functools.partial(finish, at))

    def drain(hop, count):
        spot = wbuf.at[pl.ds(0, count)]
        pltpu.make_async_remote_copy(
            src_ref=spot, dst_ref=spot, send_sem=sent.at[lane[hop]], recv_sem=recv.at[0, 0],
            device_id=(near[hop], half), device_id_type=MESH,
        ).wait_send()

    def drain_all(at):
        carried = {}
        for p, rx, ry, k in orders[at] + [(p, 0, 0, 0) for p in range(len(PARTS))]:
            for hop in hops(PARTS[p][0], rx, ry, k, at, deep):
                carried[hop] = carried.get(hop, 0) + PARTS[p][1] * unit_rows
        for hop, count in carried.items():
            drain(hop, count)

    for at in range(places):
        pl.when(place == at)(functools.partial(drain_all, at))
    for image in range(images):
        share(image).wait_send()
    for i in range(width // tile):
        cols = pl.ds(i * tile, tile)
        pltpu.make_async_copy(obuf.at[:, cols], o_hbm.at[:, cols], local.at[5 + i]).wait()


def fused(deep, inputs, queries, keys, values, out_weight):
    tokens, width = queries.shape
    rows = out_weight.shape[0]
    whole = 4 * deep * rows
    bf16, f32 = jnp.bfloat16, jnp.float32
    return pl.pallas_call(
        functools.partial(kernel, deep),
        out_shape=jax.ShapeDtypeStruct((tokens, width), bf16),
        in_specs=[pl.BlockSpec(memory_space=pl.ANY)] * 5,
        out_specs=pl.BlockSpec(memory_space=pl.ANY),
        scratch_shapes=[
            pltpu.VMEM((whole, width), bf16),
            pltpu.VMEM((tokens, width), bf16),
            pltpu.VMEM((tokens, width), bf16),
            pltpu.VMEM((tokens, width), bf16),
            pltpu.VMEM((tokens, width), bf16),
            pltpu.VMEM((tokens, whole), bf16),
            pltpu.VMEM((tokens, width), f32),
            pltpu.VMEM((tokens, width), bf16),
            pltpu.SemaphoreType.DMA((len(PARTS), 4 * deep)),
            pltpu.SemaphoreType.DMA((4,)),
            pltpu.SemaphoreType.DMA((5 + width // 256,)),
            pltpu.SemaphoreType.DMA((tokens // PATCHES,)),
            pltpu.SemaphoreType.DMA((tokens // PATCHES,)),
        ],
        compiler_params=pltpu.CompilerParams(
            collective_id=0, has_side_effects=True, vmem_limit_bytes=60 * 1024 * 1024
        ),
    )(inputs, queries, keys, values, out_weight)


def general(inputs, queries, keys, values, out_weight):
    tok_rows, local_width = queries.shape
    head_count = local_width // HEAD_DIM
    images = tok_rows // PATCHES
    split_shape = (images, PATCHES, head_count, HEAD_DIM)
    gathered = lax.all_gather(out_weight, "dp", axis=0, tiled=True)
    scores = jnp.einsum(
        "bqhd,bkhd->bhqk",
        queries.reshape(split_shape),
        keys.reshape(split_shape),
        preferred_element_type=jnp.float32,
    ) / math.sqrt(HEAD_DIM)
    row_max = jnp.max(scores, axis=-1, keepdims=True)
    shifted = jnp.exp(scores - row_max)
    probs = (shifted / jnp.sum(shifted, axis=-1, keepdims=True)).astype(jnp.bfloat16)
    attended = jnp.einsum(
        "bhqk,bkhd->bqhd", probs, values.reshape(split_shape), preferred_element_type=jnp.float32
    )
    attended = attended.astype(jnp.bfloat16).reshape(tok_rows, local_width)
    all_heads = lax.all_gather(attended, "mp", axis=1, tiled=True)
    projected = jnp.dot(all_heads, gathered, preferred_element_type=jnp.float32)
    return (inputs.astype(jnp.float32) + projected).astype(jnp.bfloat16)


def solution(mesh):
    parts, halves = mesh.shape["dp"], mesh.shape["mp"]

    def shards(inputs, queries, keys, values, out_weight):
        rows, width = out_weight.shape
        tokens = queries.shape[0]
        if (parts % 8 == 0 and 4 < parts <= 32 and halves == 2 and rows % 192 == 0 and width % 256 == 0
                and (tokens // PATCHES) * (width // HEAD_DIM) % GROUPS == 0):
            return fused(parts // 4, inputs, queries, keys, values, out_weight)
        return general(inputs, queries, keys, values, out_weight)

    return jax.shard_map(
        shards,
        mesh=mesh,
        in_specs=(P("dp", "mp"),) * 5,
        out_specs=P("dp", "mp"),
        check_vma=False,
    )
```

```python
import functools
import math

import jax
import jax.numpy as jnp
from jax import lax
from jax.experimental import pallas as pl
from jax.experimental.pallas import tpu as pltpu
from jax.sharding import PartitionSpec as P

HEAD_DIM = 128
PATCHES = 256
MESH = pl.DeviceIdType.MESH

PARTS = (("zxy", 3), ("zyx", 3), ("xzy", 3), ("yzx", 3))
GROUPS = 12
HEAD_START = 4
EARLY = (1, 2)
OWN_LATE = 0.0


def hops(order, rx, ry, k, place, deep):
    diff = {"x": rx, "y": ry, "z": k}
    last = max([i for i in range(3) if diff[order[i]]], default=-1)
    out = []
    if last >= 0 and order[last] == "z":
        out.append("i" if k < 0 else "o")
    for axis in order[last + 1:]:
        out.extend(("i", "o") if axis == "z" else (axis,))
    return [hop for hop in out if hop != "o" or place > 0]


def arrivals(deep):
    chips = [(x, y, z) for z in range(deep) for y in range(2) for x in range(2)]
    ready, busy, when = [], {}, [{} for _ in range(deep // 2)]
    for c in chips:
        for p in range(len(PARTS)):
            ready.append((0.0, p, c, c, ""))
    while ready:
        ready.sort()
        now, p, c, s, only = ready.pop(0)
        order, size = PARTS[p]
        inward = 1 if c[2] < deep // 2 else -1
        place = min(c[2], deep - 1 - c[2])
        rx, ry, k = c[0] ^ s[0], c[1] ^ s[1], (s[2] - c[2]) * inward
        if OWN_LATE and c == s and not only:
            ready.append((OWN_LATE, p, c, s, order[2]))
        if c != s:
            when[place].setdefault((p, rx, ry, k), []).append(now)
        for hop in hops(order, rx, ry, k, place, deep):
            if OWN_LATE and c == s and (only != hop if only else hop == order[2]):
                continue
            to = {
                "x": (1 - c[0], c[1], c[2]), "y": (c[0], 1 - c[1], c[2]),
                "i": (c[0], c[1], c[2] + inward), "o": (c[0], c[1], c[2] - inward),
            }[hop]
            end = max(now, busy.get((c, hop), 0.0)) + size
            busy[(c, hop)] = end
            ready.append((end + 0.3, p, to, s, ""))
    orders = [sorted(w, key=lambda e, w=w: (sum(w[e]) / len(w[e]), e)) for w in when]
    late = [sum(sum(w[e]) / len(w[e]) < OWN_LATE for e in w) for w in when]
    return orders, late


def kernel(deep, x_hbm, q_hbm, k_hbm, v_hbm, w_hbm, o_ref,
           wbuf, xin, qv, kv, vv, att, acc,
           recv, sent, local, att_sent, att_recv):
    me, half = lax.axis_index("dp"), lax.axis_index("mp")
    x, y, z = me % 2, (me // 2) % 2, me // 4
    rows, width = w_hbm.shape
    tokens = q_hbm.shape[0]
    images, heads = tokens // PATCHES, width // HEAD_DIM
    unit_rows = rows // 12
    firsts = [sum(size for _, size in PARTS[:p]) for p in range(len(PARTS))]
    places = deep // 2
    lower = z < places
    inward = jnp.where(lower, 1, -1)
    place = jnp.where(lower, z, deep - 1 - z)

    def index_of(cx, cy, cz):
        return (cz * 2 + cy) * 2 + cx

    near = {
        "x": index_of(1 - x, y, z), "y": index_of(x, 1 - y, z),
        "i": index_of(x, y, z + inward), "o": index_of(x, y, z - inward),
    }
    lane = {"x": 0, "y": 1, "i": 2, "o": 3}

    loads = [
        pltpu.make_async_copy(a, b, local.at[i])
        for i, (a, b) in enumerate(((q_hbm, qv), (k_hbm, kv), (v_hbm, vv), (x_hbm, xin)))
    ]
    own = pl.ds(pl.multiple_of(me * rows, 16), rows)
    loads.append(pltpu.make_async_copy(w_hbm, wbuf.at[own], local.at[4]))
    for load in loads:
        load.start()

    barrier = pltpu.get_barrier_semaphore()
    pl.semaphore_signal(barrier, inc=1, device_id=(me, 1 - half), device_id_type=MESH)
    for hop in "xyi":
        pl.semaphore_signal(barrier, inc=1, device_id=(near[hop], half), device_id_type=MESH)

    @pl.when(place > 0)
    def _():
        pl.semaphore_signal(barrier, inc=1, device_id=(near["o"], half), device_id_type=MESH)

    pl.semaphore_wait(barrier, 4 + jnp.minimum(place, 1))

    def piece(p, source):
        first = pl.multiple_of(source * rows + firsts[p] * unit_rows, 16)
        return wbuf.at[pl.ds(first, PARTS[p][1] * unit_rows)]

    def copy(p, source, hop, src=None):
        spot = piece(p, source)
        return pltpu.make_async_remote_copy(
            src_ref=spot if src is None else src,
            dst_ref=spot,
            send_sem=sent.at[lane[hop]],
            recv_sem=recv.at[p, source],
            device_id=(near[hop], half),
            device_id_type=MESH,
        )

    first_sends = []
    for p, (name, _) in enumerate(PARTS):
        for hop in hops(name, 0, 0, 0, 1, deep):
            first_sends.append((name.index("z" if hop in "io" else hop), p, hop))
    for _, p, hop in sorted(first_sends):
        src = w_hbm.at[pl.ds(firsts[p] * unit_rows, PARTS[p][1] * unit_rows)]
        send = copy(p, me, hop, src)
        if OWN_LATE and PARTS[p][0].index("z" if hop in "io" else hop) == 2:
            continue
        if hop == "o":
            pl.when(place > 0)(send.start)
        else:
            send.start()

    orders, late = arrivals(deep)
    seen = [0] * places

    def event(at, p, rx, ry, k):
        source = index_of((x + rx) % 2, (y + ry) % 2, z + inward * k)
        if OWN_LATE and seen[at] == late[at]:
            for own_p, (name, _) in enumerate(PARTS):
                copy(own_p, me, name[2]).start()
        seen[at] += 1
        copy(p, source, "x").wait_recv()
        for hop in hops(PARTS[p][0], rx, ry, k, at, deep):
            copy(p, source, hop).start()

    def attend(unit):
        r = pl.multiple_of((unit // heads) * PATCHES, PATCHES)
        c = pl.multiple_of((unit % heads) * HEAD_DIM, HEAD_DIM)
        here = (pl.ds(r, PATCHES), pl.ds(c, HEAD_DIM))
        s = lax.dot_general(qv[here], kv[here], (((1,), (1,)), ((), ())), preferred_element_type=jnp.float32)
        s = s * (1.0 / math.sqrt(HEAD_DIM))
        e = jnp.exp(s - jnp.max(s, axis=-1, keepdims=True))
        probs = (e / jnp.sum(e, axis=-1, keepdims=True)).astype(jnp.bfloat16)
        a = jnp.dot(probs, vv[here], preferred_element_type=jnp.float32)
        att[pl.ds(r, PATCHES), pl.ds(pl.multiple_of(half * width + c, HEAD_DIM), HEAD_DIM)] = a.astype(jnp.bfloat16)

    def share(image):
        spot = att.at[pl.ds(image * PATCHES, PATCHES), pl.ds(pl.multiple_of(half * width, HEAD_DIM), width)]
        return pltpu.make_async_remote_copy(
            src_ref=spot, dst_ref=spot, send_sem=att_sent.at[image], recv_sem=att_recv.at[image],
            device_id=(me, 1 - half), device_id_type=MESH,
        )

    block, tile = 4 * rows, 256

    def project(k, last):
        depth = pl.ds(pl.multiple_of((z + inward * k) * block, HEAD_DIM), block)

        @pl.loop(0, width // tile)
        def _(i):
            cols = pl.ds(pl.multiple_of(i * tile, tile), tile)
            start = xin[:, cols].astype(jnp.float32) if k == 0 else acc[:, cols]
            total = start + jnp.dot(att[:, depth], wbuf[depth, cols], preferred_element_type=jnp.float32)
            if last:
                o_ref[:, cols] = total.astype(jnp.bfloat16)
            else:
                acc[:, cols] = total

    for load in loads[:3] + loads[4:]:
        load.wait()

    units = images * heads
    step = units // GROUPS
    early = [len(order) * EARLY[0] // EARLY[1] for order in orders]
    done = [0] * places
    shared = 0
    for g in range(GROUPS):
        pl.loop(g * step, (g + 1) * step)(attend)
        while shared < images and (g + 1) * step >= (shared + 1) * heads:
            share(shared).start()
            shared += 1
        if g + 1 > HEAD_START:
            for at in range(places):
                upto = early[at] * (g + 1 - HEAD_START) // (GROUPS - HEAD_START)

                @pl.when(place == at)
                def _(at=at, upto=upto):
                    for e in orders[at][done[at]:upto]:
                        event(at, *e)
                done[at] = upto
    loads[3].wait()
    for image in range(images):
        share(image).wait_recv()

    def finish(at):
        rest = orders[at][done[at]:]
        final = {k: max([i for i, e in enumerate(rest) if e[3] == k], default=-1) for k in {e[3] for e in orders[at]}}
        planes = sorted(final, key=lambda k: (final[k], abs(k)))
        planes.remove(0)
        planes.insert(0, 0)
        for k in planes:
            final[k] = max(final[k], final[0])
        at_event = 0
        for k in planes:
            for e in rest[at_event:final[k] + 1]:
                event(at, *e)
            at_event = max(at_event, final[k] + 1)
            project(k, k == planes[-1])

    for at in range(places):
        pl.when(place == at)(functools.partial(finish, at))

    def drain(hop, count):
        spot = wbuf.at[pl.ds(0, count)]
        pltpu.make_async_remote_copy(
            src_ref=spot, dst_ref=spot, send_sem=sent.at[lane[hop]], recv_sem=recv.at[0, 0],
            device_id=(near[hop], half), device_id_type=MESH,
        ).wait_send()

    def drain_all(at):
        carried = {}
        for p, rx, ry, k in orders[at] + [(p, 0, 0, 0) for p in range(len(PARTS))]:
            for hop in hops(PARTS[p][0], rx, ry, k, at, deep):
                carried[hop] = carried.get(hop, 0) + PARTS[p][1] * unit_rows
        for hop, count in carried.items():
            drain(hop, count)

    for at in range(places):
        pl.when(place == at)(functools.partial(drain_all, at))
    for image in range(images):
        share(image).wait_send()


def fused(deep, inputs, queries, keys, values, out_weight):
    tokens, width = queries.shape
    rows = out_weight.shape[0]
    whole = 4 * deep * rows
    bf16, f32 = jnp.bfloat16, jnp.float32
    return pl.pallas_call(
        functools.partial(kernel, deep),
        out_shape=pltpu.VMEM((tokens, width), bf16),
        in_specs=[pl.BlockSpec(memory_space=pl.ANY)] * 5,
        out_specs=pl.BlockSpec(memory_space=pltpu.VMEM),
        scratch_shapes=[
            pltpu.VMEM((whole, width), bf16),
            pltpu.VMEM((tokens, width), bf16),
            pltpu.VMEM((tokens, width), bf16),
            pltpu.VMEM((tokens, width), bf16),
            pltpu.VMEM((tokens, width), bf16),
            pltpu.VMEM((tokens, whole), bf16),
            pltpu.VMEM((tokens, width), f32),
            pltpu.SemaphoreType.DMA((len(PARTS), 4 * deep)),
            pltpu.SemaphoreType.DMA((4,)),
            pltpu.SemaphoreType.DMA((5,)),
            pltpu.SemaphoreType.DMA((tokens // PATCHES,)),
            pltpu.SemaphoreType.DMA((tokens // PATCHES,)),
        ],
        compiler_params=pltpu.CompilerParams(
            collective_id=0, has_side_effects=True, vmem_limit_bytes=56 * 1024 * 1024
        ),
    )(inputs, queries, keys, values, out_weight)


def general(inputs, queries, keys, values, out_weight):
    tok_rows, local_width = queries.shape
    head_count = local_width // HEAD_DIM
    images = tok_rows // PATCHES
    split_shape = (images, PATCHES, head_count, HEAD_DIM)
    gathered = lax.all_gather(out_weight, "dp", axis=0, tiled=True)
    scores = jnp.einsum(
        "bqhd,bkhd->bhqk",
        queries.reshape(split_shape),
        keys.reshape(split_shape),
        preferred_element_type=jnp.float32,
    ) / math.sqrt(HEAD_DIM)
    row_max = jnp.max(scores, axis=-1, keepdims=True)
    shifted = jnp.exp(scores - row_max)
    probs = (shifted / jnp.sum(shifted, axis=-1, keepdims=True)).astype(jnp.bfloat16)
    attended = jnp.einsum(
        "bhqk,bkhd->bqhd", probs, values.reshape(split_shape), preferred_element_type=jnp.float32
    )
    attended = attended.astype(jnp.bfloat16).reshape(tok_rows, local_width)
    all_heads = lax.all_gather(attended, "mp", axis=1, tiled=True)
    projected = jnp.dot(all_heads, gathered, preferred_element_type=jnp.float32)
    return (inputs.astype(jnp.float32) + projected).astype(jnp.bfloat16)


def solution(mesh):
    parts, halves = mesh.shape["dp"], mesh.shape["mp"]

    def shards(inputs, queries, keys, values, out_weight):
        rows, width = out_weight.shape
        tokens = queries.shape[0]
        if (parts % 8 == 0 and 4 < parts <= 32 and halves == 2 and rows % 192 == 0 and width % 256 == 0
                and (tokens // PATCHES) * (width // HEAD_DIM) % GROUPS == 0):
            return fused(parts // 4, inputs, queries, keys, values, out_weight)
        return general(inputs, queries, keys, values, out_weight)

    return jax.shard_map(
        shards,
        mesh=mesh,
        in_specs=(P("dp", "mp"),) * 5,
        out_specs=P("dp", "mp"),
        check_vma=False,
    )
```

```python
import functools
import math

import jax
import jax.numpy as jnp
from jax import lax
from jax.experimental import pallas as pl
from jax.experimental.pallas import tpu as pltpu
from jax.sharding import PartitionSpec as P

HEAD_DIM = 128
PATCHES = 256
MESH = pl.DeviceIdType.MESH

PARTS = (("zxy", 3), ("zyx", 3), ("xzy", 3), ("yzx", 3))
GROUPS = 12
HEAD_START = 2
EARLY = (1, 2)
OWN_LATE = 0.0


def hops(order, rx, ry, k, place, deep):
    diff = {"x": rx, "y": ry, "z": k}
    last = max([i for i in range(3) if diff[order[i]]], default=-1)
    out = []
    if last >= 0 and order[last] == "z":
        out.append("i" if k < 0 else "o")
    for axis in order[last + 1:]:
        out.extend(("i", "o") if axis == "z" else (axis,))
    return [hop for hop in out if hop != "o" or place > 0]


def arrivals(deep):
    chips = [(x, y, z) for z in range(deep) for y in range(2) for x in range(2)]
    ready, busy, when = [], {}, [{} for _ in range(deep // 2)]
    for c in chips:
        for p in range(len(PARTS)):
            ready.append((0.0, p, c, c, ""))
    while ready:
        ready.sort()
        now, p, c, s, only = ready.pop(0)
        order, size = PARTS[p]
        inward = 1 if c[2] < deep // 2 else -1
        place = min(c[2], deep - 1 - c[2])
        rx, ry, k = c[0] ^ s[0], c[1] ^ s[1], (s[2] - c[2]) * inward
        if OWN_LATE and c == s and not only:
            ready.append((OWN_LATE, p, c, s, order[2]))
        if c != s:
            when[place].setdefault((p, rx, ry, k), []).append(now)
        for hop in hops(order, rx, ry, k, place, deep):
            if OWN_LATE and c == s and (only != hop if only else hop == order[2]):
                continue
            to = {
                "x": (1 - c[0], c[1], c[2]), "y": (c[0], 1 - c[1], c[2]),
                "i": (c[0], c[1], c[2] + inward), "o": (c[0], c[1], c[2] - inward),
            }[hop]
            end = max(now, busy.get((c, hop), 0.0)) + size
            busy[(c, hop)] = end
            ready.append((end + 0.3, p, to, s, ""))
    orders = [sorted(w, key=lambda e, w=w: (sum(w[e]) / len(w[e]), e)) for w in when]
    late = [sum(sum(w[e]) / len(w[e]) < OWN_LATE for e in w) for w in when]
    return orders, late


def kernel(deep, x_hbm, q_hbm, k_hbm, v_hbm, w_hbm, o_ref,
           wbuf, xin, qv, kv, vv, att, acc,
           recv, sent, local, att_sent, att_recv):
    me, half = lax.axis_index("dp"), lax.axis_index("mp")
    x, y, z = me % 2, (me // 2) % 2, me // 4
    rows, width = w_hbm.shape
    tokens = q_hbm.shape[0]
    images, heads = tokens // PATCHES, width // HEAD_DIM
    unit_rows = rows // 12
    firsts = [sum(size for _, size in PARTS[:p]) for p in range(len(PARTS))]
    places = deep // 2
    lower = z < places
    inward = jnp.where(lower, 1, -1)
    place = jnp.where(lower, z, deep - 1 - z)

    def index_of(cx, cy, cz):
        return (cz * 2 + cy) * 2 + cx

    near = {
        "x": index_of(1 - x, y, z), "y": index_of(x, 1 - y, z),
        "i": index_of(x, y, z + inward), "o": index_of(x, y, z - inward),
    }
    lane = {"x": 0, "y": 1, "i": 2, "o": 3}

    loads = [
        pltpu.make_async_copy(a, b, local.at[i])
        for i, (a, b) in enumerate(((q_hbm, qv), (k_hbm, kv), (v_hbm, vv), (x_hbm, xin)))
    ]
    own = pl.ds(pl.multiple_of(me * rows, 16), rows)
    loads.append(pltpu.make_async_copy(w_hbm, wbuf.at[own], local.at[4]))
    for load in loads:
        load.start()

    barrier = pltpu.get_barrier_semaphore()
    pl.semaphore_signal(barrier, inc=1, device_id=(me, 1 - half), device_id_type=MESH)
    for hop in "xyi":
        pl.semaphore_signal(barrier, inc=1, device_id=(near[hop], half), device_id_type=MESH)

    @pl.when(place > 0)
    def _():
        pl.semaphore_signal(barrier, inc=1, device_id=(near["o"], half), device_id_type=MESH)

    pl.semaphore_wait(barrier, 4 + jnp.minimum(place, 1))

    def piece(p, source):
        first = pl.multiple_of(source * rows + firsts[p] * unit_rows, 16)
        return wbuf.at[pl.ds(first, PARTS[p][1] * unit_rows)]

    def copy(p, source, hop, src=None):
        spot = piece(p, source)
        return pltpu.make_async_remote_copy(
            src_ref=spot if src is None else src,
            dst_ref=spot,
            send_sem=sent.at[lane[hop]],
            recv_sem=recv.at[p, source],
            device_id=(near[hop], half),
            device_id_type=MESH,
        )

    first_sends = []
    for p, (name, _) in enumerate(PARTS):
        for hop in hops(name, 0, 0, 0, 1, deep):
            first_sends.append((name.index("z" if hop in "io" else hop), p, hop))
    for _, p, hop in sorted(first_sends):
        src = w_hbm.at[pl.ds(firsts[p] * unit_rows, PARTS[p][1] * unit_rows)]
        send = copy(p, me, hop, src)
        if OWN_LATE and PARTS[p][0].index("z" if hop in "io" else hop) == 2:
            continue
        if hop == "o":
            pl.when(place > 0)(send.start)
        else:
            send.start()

    orders, late = arrivals(deep)
    seen = [0] * places

    def event(at, p, rx, ry, k):
        source = index_of((x + rx) % 2, (y + ry) % 2, z + inward * k)
        if OWN_LATE and seen[at] == late[at]:
            for own_p, (name, _) in enumerate(PARTS):
                copy(own_p, me, name[2]).start()
        seen[at] += 1
        copy(p, source, "x").wait_recv()
        for hop in hops(PARTS[p][0], rx, ry, k, at, deep):
            copy(p, source, hop).start()

    def attend(unit):
        r = pl.multiple_of((unit // heads) * PATCHES, PATCHES)
        c = pl.multiple_of((unit % heads) * HEAD_DIM, HEAD_DIM)
        here = (pl.ds(r, PATCHES), pl.ds(c, HEAD_DIM))
        s = lax.dot_general(qv[here], kv[here], (((1,), (1,)), ((), ())), preferred_element_type=jnp.float32)
        s = s * (1.0 / math.sqrt(HEAD_DIM))
        e = jnp.exp(s - jnp.max(s, axis=-1, keepdims=True))
        probs = (e / jnp.sum(e, axis=-1, keepdims=True)).astype(jnp.bfloat16)
        a = jnp.dot(probs, vv[here], preferred_element_type=jnp.float32)
        att[pl.ds(r, PATCHES), pl.ds(pl.multiple_of(half * width + c, HEAD_DIM), HEAD_DIM)] = a.astype(jnp.bfloat16)

    def share(image):
        spot = att.at[pl.ds(image * PATCHES, PATCHES), pl.ds(pl.multiple_of(half * width, HEAD_DIM), width)]
        return pltpu.make_async_remote_copy(
            src_ref=spot, dst_ref=spot, send_sem=att_sent.at[image], recv_sem=att_recv.at[image],
            device_id=(me, 1 - half), device_id_type=MESH,
        )

    block, tile = 4 * rows, 256

    def project(k, last):
        depth = pl.ds(pl.multiple_of((z + inward * k) * block, HEAD_DIM), block)

        @pl.loop(0, width // tile)
        def _(i):
            cols = pl.ds(pl.multiple_of(i * tile, tile), tile)
            start = xin[:, cols].astype(jnp.float32) if k == 0 else acc[:, cols]
            total = start + jnp.dot(att[:, depth], wbuf[depth, cols], preferred_element_type=jnp.float32)
            if last:
                o_ref[:, cols] = total.astype(jnp.bfloat16)
            else:
                acc[:, cols] = total

    for load in loads[:3] + loads[4:]:
        load.wait()

    units = images * heads
    step = units // GROUPS
    early = [len(order) * EARLY[0] // EARLY[1] for order in orders]
    done = [0] * places
    shared = 0
    for g in range(GROUPS):
        pl.loop(g * step, (g + 1) * step)(attend)
        while shared < images and (g + 1) * step >= (shared + 1) * heads:
            share(shared).start()
            shared += 1
        if g + 1 > HEAD_START:
            for at in range(places):
                upto = early[at] * (g + 1 - HEAD_START) // (GROUPS - HEAD_START)

                @pl.when(place == at)
                def _(at=at, upto=upto):
                    for e in orders[at][done[at]:upto]:
                        event(at, *e)
                done[at] = upto
    loads[3].wait()
    for image in range(images):
        share(image).wait_recv()

    def finish(at):
        rest = orders[at][done[at]:]
        final = {k: max([i for i, e in enumerate(rest) if e[3] == k], default=-1) for k in {e[3] for e in orders[at]}}
        planes = sorted(final, key=lambda k: (final[k], abs(k)))
        planes.remove(0)
        planes.insert(0, 0)
        for k in planes:
            final[k] = max(final[k], final[0])
        at_event = 0
        for k in planes:
            for e in rest[at_event:final[k] + 1]:
                event(at, *e)
            at_event = max(at_event, final[k] + 1)
            project(k, k == planes[-1])

    for at in range(places):
        pl.when(place == at)(functools.partial(finish, at))

    def drain(hop, count):
        spot = wbuf.at[pl.ds(0, count)]
        pltpu.make_async_remote_copy(
            src_ref=spot, dst_ref=spot, send_sem=sent.at[lane[hop]], recv_sem=recv.at[0, 0],
            device_id=(near[hop], half), device_id_type=MESH,
        ).wait_send()

    def drain_all(at):
        carried = {}
        for p, rx, ry, k in orders[at] + [(p, 0, 0, 0) for p in range(len(PARTS))]:
            for hop in hops(PARTS[p][0], rx, ry, k, at, deep):
                carried[hop] = carried.get(hop, 0) + PARTS[p][1] * unit_rows
        for hop, count in carried.items():
            drain(hop, count)

    for at in range(places):
        pl.when(place == at)(functools.partial(drain_all, at))
    for image in range(images):
        share(image).wait_send()


def fused(deep, inputs, queries, keys, values, out_weight):
    tokens, width = queries.shape
    rows = out_weight.shape[0]
    whole = 4 * deep * rows
    bf16, f32 = jnp.bfloat16, jnp.float32
    return pl.pallas_call(
        functools.partial(kernel, deep),
        out_shape=pltpu.VMEM((tokens, width), bf16),
        in_specs=[pl.BlockSpec(memory_space=pl.ANY)] * 5,
        out_specs=pl.BlockSpec(memory_space=pltpu.VMEM),
        scratch_shapes=[
            pltpu.VMEM((whole, width), bf16),
            pltpu.VMEM((tokens, width), bf16),
            pltpu.VMEM((tokens, width), bf16),
            pltpu.VMEM((tokens, width), bf16),
            pltpu.VMEM((tokens, width), bf16),
            pltpu.VMEM((tokens, whole), bf16),
            pltpu.VMEM((tokens, width), f32),
            pltpu.SemaphoreType.DMA((len(PARTS), 4 * deep)),
            pltpu.SemaphoreType.DMA((4,)),
            pltpu.SemaphoreType.DMA((5,)),
            pltpu.SemaphoreType.DMA((tokens // PATCHES,)),
            pltpu.SemaphoreType.DMA((tokens // PATCHES,)),
        ],
        compiler_params=pltpu.CompilerParams(
            collective_id=0, has_side_effects=True, vmem_limit_bytes=56 * 1024 * 1024
        ),
    )(inputs, queries, keys, values, out_weight)


def general(inputs, queries, keys, values, out_weight):
    tok_rows, local_width = queries.shape
    head_count = local_width // HEAD_DIM
    images = tok_rows // PATCHES
    split_shape = (images, PATCHES, head_count, HEAD_DIM)
    gathered = lax.all_gather(out_weight, "dp", axis=0, tiled=True)
    scores = jnp.einsum(
        "bqhd,bkhd->bhqk",
        queries.reshape(split_shape),
        keys.reshape(split_shape),
        preferred_element_type=jnp.float32,
    ) / math.sqrt(HEAD_DIM)
    row_max = jnp.max(scores, axis=-1, keepdims=True)
    shifted = jnp.exp(scores - row_max)
    probs = (shifted / jnp.sum(shifted, axis=-1, keepdims=True)).astype(jnp.bfloat16)
    attended = jnp.einsum(
        "bhqk,bkhd->bqhd", probs, values.reshape(split_shape), preferred_element_type=jnp.float32
    )
    attended = attended.astype(jnp.bfloat16).reshape(tok_rows, local_width)
    all_heads = lax.all_gather(attended, "mp", axis=1, tiled=True)
    projected = jnp.dot(all_heads, gathered, preferred_element_type=jnp.float32)
    return (inputs.astype(jnp.float32) + projected).astype(jnp.bfloat16)


def solution(mesh):
    parts, halves = mesh.shape["dp"], mesh.shape["mp"]

    def shards(inputs, queries, keys, values, out_weight):
        rows, width = out_weight.shape
        tokens = queries.shape[0]
        if (parts % 8 == 0 and 4 < parts <= 32 and halves == 2 and rows % 192 == 0 and width % 256 == 0
                and (tokens // PATCHES) * (width // HEAD_DIM) % GROUPS == 0):
            return fused(parts // 4, inputs, queries, keys, values, out_weight)
        return general(inputs, queries, keys, values, out_weight)

    return jax.shard_map(
        shards,
        mesh=mesh,
        in_specs=(P("dp", "mp"),) * 5,
        out_specs=P("dp", "mp"),
        check_vma=False,
    )
```
